32 devices in a mesh: row: 8 (over z, core), col: 4 (over y, x).
Axes of the slice: x: 2, y: 2, z: 4, core: 2. Of those that a mesh axis runs over, the one named last changes fastest.
Arguments:
- features: bfloat16 [4096, 128], P(('row', 'col')), may hold values from -6 to 6
- weight: bfloat16 [128, 256], replicated, may hold values from -0.5 to 0.5
- bias: float32 [256], replicated, may hold values from -3 to 3
- tiles: bfloat16 [8, 4, 8, 512, 512], P('row', 'col'), may hold values from -0.125 to 0.125
- tile_rows: int32 [8, 4, 8], P('row', 'col'), may hold values from 0 to 0
- tile_cols: int32 [8, 4, 8], P('row', 'col'), may hold values from 0 to 1
- tile_counts: int32 [8, 4], P('row', 'col'), may hold values from 1 to 8, as said below
- cotangent: bfloat16 [4096, 256], P(('row', 'col')), may hold values from -6 to 6
Outputs:
- output: bfloat16 [4096, 256], P(('row', 'col'))
- grad_features: bfloat16 [4096, 128], P(('row', 'col'))
- grad_weight: float32 [128, 256], replicated
- grad_bias: float32 [256], replicated
The draws below stay inside these ranges and needn't reach their ends.
Inputs may be any that keep to these rules, and one draw needn't show every extreme that they name: `tile_counts`: some device has all 8 slots live.
All inputs are finite; a program needn't handle non-finite values.
Results may differ from the reference program's by a relative error of at most 0.02.
Values may be sent and summed in bfloat16 or wider, within the bound.
A program may use at most 64 MiB of HBM per device.

```python
import jax
import jax.numpy as jnp
from jax import lax

F = 128
H = 256
TILE = 512
CAP = 8
NODES_DEV = 128
NODES = 4096
N_ROW = 8
N_COL = 4


def draw_tile_rows(key, part):
    key = jax.random.fold_in(key, 11)
    return jax.random.randint(key, (N_ROW, N_COL, CAP), 0, N_COL * NODES_DEV // TILE).astype(jnp.int32)


def draw_tile_cols(key, part):
    key = jax.random.fold_in(key, 12)
    return jax.random.randint(key, (N_ROW, N_COL, CAP), 0, N_ROW * NODES_DEV // TILE).astype(jnp.int32)


def draw_tile_counts(key, part):
    key = jax.random.fold_in(key, 13)
    first_key, second_key, third_key = jax.random.split(key, 3)
    base_counts = jax.random.randint(first_key, (N_ROW * N_COL,), 1, 5)
    heavy = jax.random.randint(second_key, (N_ROW * N_COL,), 0, 8) == 0
    counts = jnp.where(heavy, CAP, base_counts)
    chosen = jax.random.randint(third_key, (), 0, N_ROW * N_COL)
    counts = counts.at[chosen].set(CAP)
    return counts.reshape(N_ROW, N_COL).astype(jnp.int32)


def block_levels(rng, extent, shards, smallest, largest):
    factor_of, own = 1.0, jax.random.fold_in(rng, 6)
    for axis_at, parts in shards:
        heights = jnp.exp(jax.random.uniform(jax.random.fold_in(own, axis_at), (parts,), jnp.float32, smallest / len(shards), largest / len(shards)))
        factor_of = factor_of * jnp.repeat(heights, extent[axis_at] // parts).reshape([-1 if axis == axis_at else 1 for axis in range(len(extent))])
    return factor_of


def centred(own_key, dims, scale, reach, shards=(), kind=jnp.bfloat16):
    gain = block_levels(own_key, dims, shards, -0.22, 0.18) if shards else 1.0
    drawn = jax.random.normal(own_key, dims, jnp.float32) * scale * gain
    return jnp.minimum(jnp.maximum(drawn, -reach), reach).astype(kind)


def setup_inputs(seed: int = 0) -> dict:
    key_of = jax.random.split(jax.random.key(seed), 9)
    return {
        "features": centred(key_of[0], (NODES, F), 1.0, 6.0, ((0, 32),)),
        "weight": centred(key_of[1], (F, H), F ** -0.5, 0.5),
        "bias": centred(key_of[2], (H,), 0.5, 3.0, (), jnp.float32),
        "tiles": centred(key_of[3], (N_ROW, N_COL, CAP, TILE, TILE), (4 * TILE) ** -0.5, 0.125, ((0, 8), (1, 4))),
        "tile_rows": draw_tile_rows(jax.random.fold_in(key_of[8], 71), 0),
        "tile_cols": draw_tile_cols(jax.random.fold_in(key_of[8], 71), 0),
        "tile_counts": draw_tile_counts(jax.random.fold_in(key_of[8], 71), 0),
        "cotangent": centred(key_of[7], (NODES, H), 1.0, 6.0, ((0, 32),)),
    }


def silu_parts(pre_act):
    sigmoid_val = jax.nn.sigmoid(pre_act)
    return pre_act * sigmoid_val, sigmoid_val * (1.0 + pre_act * (1.0 - sigmoid_val))


def round_keep(block_sum):
    rounded = lax.optimization_barrier(block_sum.astype(jnp.bfloat16))
    return rounded.astype(jnp.float32)


def reference(features, weight, bias, tiles, tile_rows, tile_cols, tile_counts, cotangent):
    block_len = N_COL * NODES_DEV
    panel_len = N_ROW * NODES_DEV
    row_tiles = block_len // TILE
    col_tiles = panel_len // TILE
    slot_ids = jnp.arange(CAP, dtype=jnp.int32)
    projected = jnp.dot(features, weight, preferred_element_type=jnp.float32).astype(jnp.bfloat16)
    panels = projected.reshape(N_ROW, N_COL, NODES_DEV, H).transpose(1, 0, 2, 3).reshape(N_COL, col_tiles, TILE, H)

    def forward_term(row_idx, col_idx):
        is_live = (slot_ids < tile_counts[row_idx, col_idx]).astype(jnp.float32)
        picked = panels[col_idx][tile_cols[row_idx, col_idx]].astype(jnp.float32)
        product = jnp.einsum("ktj,kjh->kth", tiles[row_idx, col_idx].astype(jnp.float32), picked)
        placer = (tile_rows[row_idx, col_idx][:, None] == jnp.arange(row_tiles, dtype=jnp.int32)[None, :]).astype(jnp.float32) * is_live[:, None]
        return round_keep(jnp.einsum("kr,kth->rth", placer, product).reshape(block_len, H))

    def block_row(row_idx):
        def step_fn(total_sum, col_idx):
            return total_sum + forward_term(row_idx, col_idx), None
        total_sum, _ = lax.scan(step_fn, jnp.zeros((block_len, H), jnp.float32), jnp.arange(N_COL, dtype=jnp.int32))
        return total_sum

    aggregate = lax.map(block_row, jnp.arange(N_ROW, dtype=jnp.int32)).reshape(NODES, H)
    pre_act = aggregate + bias
    activated, derivative = silu_parts(pre_act)
    output = activated.astype(jnp.bfloat16)
    grad_pre = (cotangent.astype(jnp.float32) * derivative).astype(jnp.bfloat16)
    grad_blocks = grad_pre.reshape(N_ROW, row_tiles, TILE, H)

    def backward_term(row_idx, col_idx):
        is_live = (slot_ids < tile_counts[row_idx, col_idx]).astype(jnp.float32)
        picked = grad_blocks[row_idx][tile_rows[row_idx, col_idx]].astype(jnp.float32)
        product = jnp.einsum("ktj,kth->kjh", tiles[row_idx, col_idx].astype(jnp.float32), picked)
        placer = (tile_cols[row_idx, col_idx][:, None] == jnp.arange(col_tiles, dtype=jnp.int32)[None, :]).astype(jnp.float32) * is_live[:, None]
        return round_keep(jnp.einsum("kr,kjh->rjh", placer, product).reshape(panel_len, H))

    def col_panel(col_idx):
        def step_fn(total_sum, row_idx):
            return total_sum + backward_term(row_idx, col_idx), None
        total_sum, _ = lax.scan(step_fn, jnp.zeros((panel_len, H), jnp.float32), jnp.arange(N_ROW, dtype=jnp.int32))
        return total_sum

    grad_panels = lax.map(col_panel, jnp.arange(N_COL, dtype=jnp.int32))
    grad_projected = grad_panels.reshape(N_COL, N_ROW, NODES_DEV, H).transpose(1, 0, 2, 3).reshape(NODES, H).astype(jnp.bfloat16)
    grad_features = jnp.dot(grad_projected, weight.T, preferred_element_type=jnp.float32).astype(jnp.bfloat16)
    grad_weight = jnp.dot(features.T, grad_projected, preferred_element_type=jnp.float32)
    grad_bias = jnp.sum(grad_pre.astype(jnp.float32), axis=0)
    return output, grad_features, grad_weight, grad_bias
```

```python
import functools

import jax
import jax.numpy as jnp
from jax import lax
from jax.experimental import pallas as pl
from jax.experimental.pallas import tpu as pltpu
from jax.sharding import PartitionSpec as P

F32, BF16 = jnp.float32, jnp.bfloat16
EXTRA = 16
CHUNK = 16


def kernel(
    n_row, n_col, fused_weight,
    feat_hbm, weight_hbm, bias_hbm, tiles_hbm, rows_ref, cols_ref, counts_ref, cot_hbm,
    out_hbm, gf_hbm, gw_hbm, gb_hbm,
    tile_buf, adj, panel, weight, bias, cot, part, part_in, z_buf, back, back_in,
    gw_own, gw_in, gw_mid, gw_all, out_st, gf_st, gw_st, gb_st,
    tile_sem, load_sem, store_sem, send_sem, recv_sem,
):
    my_row, my_col = lax.axis_index("row"), lax.axis_index("col")
    nodes, feat = feat_hbm.shape
    hidden = weight.shape[1]
    slots, tile_len = tile_buf.shape[0], tile_buf.shape[1]
    row_tiles, col_tiles = adj.shape[0] // tile_len, adj.shape[1] // tile_len
    row_peers = [lax.rem(my_row + d, n_row) for d in range(1, n_row)]
    col_peers = [lax.rem(my_col + d, n_col) for d in range(1, n_col)]

    def at_row(peer):
        return (peer, my_col)

    def at_col(peer):
        return (my_row, peer)

    tile_parts = tile_sem.shape[0]
    part_rows = tile_len // tile_parts
    tile_loads = [
        pltpu.make_async_copy(
            tiles_hbm.at[0, 0, :, pl.ds(j * part_rows, part_rows), :],
            tile_buf.at[:, pl.ds(j * part_rows, part_rows), :],
            tile_sem.at[j],
        )
        for j in range(tile_parts)
    ]
    own_rows = pl.ds(pl.multiple_of(my_row * nodes, nodes), nodes)
    loads = [
        pltpu.make_async_copy(feat_hbm, panel.at[own_rows, :], load_sem.at[0]),
        pltpu.make_async_copy(weight_hbm, weight, load_sem.at[1]),
        pltpu.make_async_copy(bias_hbm, bias, load_sem.at[2]),
        pltpu.make_async_copy(cot_hbm, cot, load_sem.at[3]),
    ]
    barrier = pltpu.get_barrier_semaphore()
    for peer in row_peers:
        pl.semaphore_signal(barrier, inc=1, device_id=at_row(peer), device_id_type=pl.DeviceIdType.MESH)
    for peer in col_peers:
        pl.semaphore_signal(barrier, inc=1, device_id=at_col(peer), device_id_type=pl.DeviceIdType.MESH)
    for copy in tile_loads + loads:
        copy.start()
    pl.semaphore_wait(barrier, n_row + n_col - 2)

    def send(src, dst, phase, target):
        copy = pltpu.make_async_remote_copy(
            src_ref=src, dst_ref=dst, send_sem=send_sem.at[phase], recv_sem=recv_sem.at[phase],
            device_id=target, device_id_type=pl.DeviceIdType.MESH,
        )
        copy.start()

    def wait_in(ref, phase):
        pltpu.make_async_copy(ref, ref, recv_sem.at[phase]).wait()

    def wait_out(ref, phase):
        pltpu.make_async_copy(ref, ref, send_sem.at[phase]).wait()

    for peer in row_peers:
        send(feat_hbm, panel.at[own_rows, :], 0, at_row(peer))

    count = counts_ref[0, 0]
    group = 2 if col_tiles % 2 == 0 else 1
    groups = row_tiles * col_tiles // group

    def densify(tile_row, first_col, start, steps):
        gains = []
        for k in range(slots):
            live = jnp.logical_and(k < count, rows_ref[0, 0, k] == tile_row)
            col = cols_ref[0, 0, k]
            gains.append([
                jnp.where(jnp.logical_and(live, col == first_col + g), 1.0, 0.0).astype(F32)
                for g in range(group)
            ])

        def step(i, carry):
            at = pl.multiple_of(start + i * CHUNK, CHUNK)
            totals = [jnp.zeros((CHUNK, tile_len), F32) for _ in range(group)]
            for k in range(slots):
                block = tile_buf[k, pl.ds(at, CHUNK), :].astype(F32)
                totals = [total + block * gains[k][g] for g, total in enumerate(totals)]
            for g, total in enumerate(totals):
                rows = pl.ds(pl.multiple_of(tile_row * tile_len + at, CHUNK), CHUNK)
                lanes = pl.ds(pl.multiple_of((first_col + g) * tile_len, tile_len), tile_len)
                adj[rows, lanes] = total.astype(BF16)
            return carry

        lax.fori_loop(0, steps, step, 0)

    if groups == 1:
        for j in range(tile_parts):
            tile_loads[j].wait()
            densify(0, 0, j * part_rows, part_rows // CHUNK)
    else:
        for j in range(tile_parts):
            tile_loads[j].wait()

        def one_group(i, carry):
            per_row = col_tiles // group
            densify(i // per_row, lax.rem(i, per_row) * group, 0, tile_len // CHUNK)
            return carry

        lax.fori_loop(0, groups, one_group, 0)

    for copy in loads:
        copy.wait()
    wait_in(panel.at[pl.ds(0, (n_row - 1) * nodes), :], 0)
    for c in range(n_col):
        part[c] = jnp.dot(
            adj[c * nodes:(c + 1) * nodes, :], panel[...], preferred_element_type=F32
        ).astype(BF16)
    for peer in col_peers:
        send(part.at[peer], part_in.at[my_col], 1, at_col(peer))
    part_in[my_col] = part[my_col]
    wait_in(part_in.at[pl.ds(0, n_col - 1)], 1)
    mixed = part_in[0].astype(F32)
    for c in range(1, n_col):
        mixed = mixed + part_in[c].astype(F32)
    mixed = mixed.astype(BF16)

    pre_act = jnp.dot(mixed, weight[...], preferred_element_type=F32) + bias[...]
    sig = jax.nn.sigmoid(pre_act)
    grad_pre = (cot[...].astype(F32) * (sig * (1.0 + pre_act * (1.0 - sig)))).astype(BF16)
    z_own = lax.dot_general(weight[...], grad_pre, (((1,), (1,)), ((), ())), preferred_element_type=F32)
    own_lanes = pl.ds(pl.multiple_of(my_col * nodes, nodes), nodes)
    z_buf[0:feat, own_lanes] = z_own.astype(BF16)
    gb_local = jnp.sum(grad_pre.astype(F32), axis=0, keepdims=True)
    halves = [gb_local[:, i * nodes:(i + 1) * nodes] for i in range(hidden // nodes)]
    n_half = len(halves)
    high = [half.astype(BF16).astype(F32) for half in halves]
    low = [half - top for half, top in zip(halves, high)]
    pad = jnp.zeros((EXTRA - 2 * n_half, nodes), F32)
    z_buf[feat:feat + EXTRA, own_lanes] = jnp.concatenate(high + low + [pad], axis=0).astype(BF16)
    for peer in col_peers:
        send(z_buf.at[:, own_lanes], z_buf.at[:, own_lanes], 2, at_col(peer))
    gw_local = lax.dot_general(mixed, grad_pre, (((0,), (0,)), ((), ())), preferred_element_type=F32)
    if fused_weight:
        share = feat // n_row
        gw_own[...] = gw_local.astype(BF16).reshape(n_row, share, hidden)
        for peer in row_peers:
            send(gw_own.at[peer], gw_in.at[my_row], 4, at_row(peer))
        gw_in[my_row] = gw_own[my_row]
    else:
        gw_st[...] = gw_local
    out_st[...] = (pre_act * sig).astype(BF16)
    out_store = pltpu.make_async_copy(out_st, out_hbm, store_sem.at[0])
    out_store.start()

    wait_in(z_buf.at[:, pl.ds(0, (n_col - 1) * nodes)], 2)
    gb_block = z_buf[feat:feat + EXTRA, 0:nodes].astype(F32)
    for c in range(1, n_col):
        gb_block = gb_block + z_buf[feat:feat + EXTRA, c * nodes:(c + 1) * nodes].astype(F32)
    halves = [gb_block[i:i + 1, :] + gb_block[n_half + i:n_half + i + 1, :] for i in range(n_half)]
    high = [half.astype(BF16).astype(F32) for half in halves]
    low = [half - top for half, top in zip(halves, high)]
    gb_rows = jnp.concatenate(high + low + [pad], axis=0).astype(BF16)
    for r in range(n_row):
        back[r, 0:feat, :] = jnp.dot(
            z_buf[0:feat, :], adj[:, r * nodes:(r + 1) * nodes], preferred_element_type=F32
        ).astype(BF16)
        back[r, feat:feat + EXTRA, :] = gb_rows
    for peer in row_peers:
        send(back.at[peer], back_in.at[my_row], 3, at_row(peer))
    back_in[my_row] = back[my_row]

    if fused_weight:
        wait_in(gw_in.at[pl.ds(0, n_row - 1)], 4)
        gw_sum = gw_in[0].astype(F32)
        for r in range(1, n_row):
            gw_sum = gw_sum + gw_in[r].astype(F32)
        gw_mid[my_col] = gw_sum.astype(BF16)
        for peer in col_peers:
            send(gw_mid.at[my_col], gw_mid.at[my_col], 5, at_col(peer))
        wait_in(gw_mid.at[pl.ds(0, n_col - 1)], 5)
        gw_sum = gw_mid[0].astype(F32)
        for c in range(1, n_col):
            gw_sum = gw_sum + gw_mid[c].astype(F32)
        gw_all[my_row] = gw_sum.astype(BF16)
        for peer in row_peers:
            send(gw_all.at[my_row], gw_all.at[my_row], 6, at_row(peer))

    wait_in(back_in.at[pl.ds(0, n_row - 1)], 3)
    total = back_in[0].astype(F32)
    for r in range(1, n_row):
        total = total + back_in[r].astype(F32)
    gf_st[...] = total[0:feat, :].T.astype(BF16)
    gf_store = pltpu.make_async_copy(gf_st, gf_hbm, store_sem.at[1])
    gf_store.start()
    for i in range(n_half):
        gb_st[:, i * nodes:(i + 1) * nodes] = (
            total[feat + i:feat + i + 1, :] + total[feat + n_half + i:feat + n_half + i + 1, :]
        )
    gb_store = pltpu.make_async_copy(gb_st, gb_hbm, store_sem.at[2])
    gb_store.start()
    if fused_weight:
        wait_in(gw_all.at[pl.ds(0, n_row - 1)], 6)
        gw_st[...] = gw_all[...].astype(F32).reshape(feat, hidden)
    gw_store = pltpu.make_async_copy(gw_st, gw_hbm, store_sem.at[3])
    gw_store.start()

    wait_out(panel.at[pl.ds(0, (n_row - 1) * nodes), :], 0)
    wait_out(part_in.at[pl.ds(0, n_col - 1)], 1)
    wait_out(z_buf.at[:, pl.ds(0, (n_col - 1) * nodes)], 2)
    wait_out(back_in.at[pl.ds(0, n_row - 1)], 3)
    if fused_weight:
        wait_out(gw_in.at[pl.ds(0, n_row - 1)], 4)
        wait_out(gw_mid.at[pl.ds(0, n_col - 1)], 5)
        wait_out(gw_all.at[pl.ds(0, n_row - 1)], 6)
    for store in (out_store, gf_store, gb_store, gw_store):
        store.wait()


def shards(n_row, n_col, features, weight, bias, tiles, tile_rows, tile_cols, tile_counts, cotangent):
    nodes, feat = features.shape
    hidden = weight.shape[1]
    slots, tile_len = tiles.shape[2], tiles.shape[3]
    block_len, panel_len = nodes * n_col, nodes * n_row
    fused_weight = feat % (n_row * 16) == 0
    share = feat // n_row if fused_weight else 16
    hbm = pl.BlockSpec(memory_space=pl.ANY)
    smem = pl.BlockSpec(memory_space=pltpu.SMEM)
    out, gf, gw, gb = pl.pallas_call(
        functools.partial(kernel, n_row, n_col, fused_weight),
        out_shape=(
            jax.ShapeDtypeStruct((nodes, hidden), BF16),
            jax.ShapeDtypeStruct((nodes, feat), BF16),
            jax.ShapeDtypeStruct((feat, hidden), F32),
            jax.ShapeDtypeStruct((1, hidden), F32),
        ),
        in_specs=[hbm, hbm, hbm, hbm, smem, smem, smem, hbm],
        out_specs=(hbm, hbm, hbm, hbm),
        scratch_shapes=[
            pltpu.VMEM((slots, tile_len, tile_len), BF16),
            pltpu.VMEM((block_len, panel_len), BF16),
            pltpu.VMEM((panel_len, feat), BF16),
            pltpu.VMEM((feat, hidden), BF16),
            pltpu.VMEM((1, hidden), F32),
            pltpu.VMEM((nodes, hidden), BF16),
            pltpu.VMEM((n_col, nodes, feat), BF16),
            pltpu.VMEM((n_col, nodes, feat), BF16),
            pltpu.VMEM((feat + EXTRA, block_len), BF16),
            pltpu.VMEM((n_row, feat + EXTRA, nodes), BF16),
            pltpu.VMEM((n_row, feat + EXTRA, nodes), BF16),
            pltpu.VMEM((n_row, share, hidden), BF16),
            pltpu.VMEM((n_row, share, hidden), BF16),
            pltpu.VMEM((n_col, share, hidden), BF16),
            pltpu.VMEM((n_row, share, hidden), BF16),
            pltpu.VMEM((nodes, hidden), BF16),
            pltpu.VMEM((nodes, feat), BF16),
            pltpu.VMEM((feat, hidden), F32),
            pltpu.VMEM((1, hidden), F32),
            pltpu.SemaphoreType.DMA((4,)),
            pltpu.SemaphoreType.DMA((4,)),
            pltpu.SemaphoreType.DMA((4,)),
            pltpu.SemaphoreType.DMA((7,)),
            pltpu.SemaphoreType.DMA((7,)),
        ],
        compiler_params=pltpu.CompilerParams(
            collective_id=0, has_side_effects=True, vmem_limit_bytes=48 * 1024 * 1024
        ),
    )(features, weight, bias.reshape(1, hidden), tiles, tile_rows, tile_cols, tile_counts, cotangent)
    gb = gb.reshape(hidden)
    if not fused_weight:
        gw = lax.psum(gw, ("row", "col"))
    return out, gf, gw, gb


def solution(mesh):
    return jax.shard_map(
        functools.partial(shards, mesh.shape["row"], mesh.shape["col"]),
        mesh=mesh,
        in_specs=(
            P(("row", "col"), None),
            P(),
            P(),
            P("row", "col", None, None, None),
            P("row", "col", None),
            P("row", "col", None),
            P("row", "col"),
            P(("row", "col"), None),
        ),
        out_specs=(P(("row", "col"), None), P(("row", "col"), None), P(), P()),
        check_vma=False,
    )
```

```python
import functools

import jax
import jax.numpy as jnp
from jax import lax
from jax.experimental import pallas as pl
from jax.experimental.pallas import tpu as pltpu
from jax.sharding import PartitionSpec as P

F32, BF16 = jnp.float32, jnp.bfloat16
EXTRA = 16
CHUNK = 16


def kernel(
    n_row, n_col, fused_weight,
    feat_hbm, weight_hbm, bias_hbm, tiles_hbm, rows_hbm, cols_hbm, counts_ref, cot_hbm,
    out_st, gf_st, gw_st, gb_st,
    tile_buf, adj, panel, weight, bias, cot, part, part_in, z_buf, back, back_in,
    pair_in, back_out, gw_own, gw_in, gw_mid, gw_all,
    rows_ref, cols_ref, tile_sem, load_sem, send_sem, recv_sem, hop_sem,
):
    my_row, my_col = lax.axis_index("row"), lax.axis_index("col")
    nodes, feat = feat_hbm.shape
    hidden = weight.shape[1]
    slots, tile_len = tile_buf.shape[0], tile_buf.shape[1]
    row_tiles, col_tiles = adj.shape[0] // tile_len, adj.shape[1] // tile_len
    row_peers = [lax.rem(my_row + d, n_row) for d in range(1, n_row)]
    col_peers = [lax.rem(my_col + d, n_col) for d in range(1, n_col)]

    pairs = n_row // 2
    pair, side = my_row // 2, lax.rem(my_row, 2)
    other = 1 - side
    sibling = pair * 2 + other
    pair_peers = [lax.rem(pair + d, pairs) for d in range(1, pairs)]

    def at_row(peer):
        return (peer, my_col)

    def at_col(peer):
        return (my_row, peer)

    tile_parts = tile_sem.shape[0]
    part_rows = tile_len // tile_parts
    tile_loads = [
        pltpu.make_async_copy(
            tiles_hbm.at[0, 0, :, pl.ds(j * part_rows, part_rows), :],
            tile_buf.at[:, pl.ds(j * part_rows, part_rows), :],
            tile_sem.at[j],
        )
        for j in range(tile_parts)
    ]
    own_rows = pl.ds(pl.multiple_of(my_row * nodes, nodes), nodes)
    loads = [
        pltpu.make_async_copy(feat_hbm, panel.at[own_rows, :], load_sem.at[0]),
        pltpu.make_async_copy(weight_hbm, weight, load_sem.at[1]),
        pltpu.make_async_copy(bias_hbm, bias, load_sem.at[2]),
        pltpu.make_async_copy(cot_hbm, cot, load_sem.at[3]),
    ]
    slot_loads = [
        pltpu.make_async_copy(rows_hbm, rows_ref, load_sem.at[4]),
        pltpu.make_async_copy(cols_hbm, cols_ref, load_sem.at[5]),
    ]
    barrier = pltpu.get_barrier_semaphore()
    for peer in row_peers:
        pl.semaphore_signal(barrier, inc=1, device_id=at_row(peer), device_id_type=pl.DeviceIdType.MESH)
    for peer in col_peers:
        pl.semaphore_signal(barrier, inc=1, device_id=at_col(peer), device_id_type=pl.DeviceIdType.MESH)
    for copy in slot_loads + tile_loads + loads:
        copy.start()
    pl.semaphore_wait(barrier, n_row + n_col - 2)

    def send(src, dst, phase, target, landed=None):
        copy = pltpu.make_async_remote_copy(
            src_ref=src, dst_ref=dst, send_sem=send_sem.at[phase],
            recv_sem=recv_sem.at[phase] if landed is None else landed,
            device_id=target, device_id_type=pl.DeviceIdType.MESH,
        )
        copy.start()

    def wait_in(ref, phase):
        pltpu.make_async_copy(ref, ref, recv_sem.at[phase]).wait()

    def wait_out(ref, phase):
        pltpu.make_async_copy(ref, ref, send_sem.at[phase]).wait()

    for d, peer in enumerate(pair_peers):
        send(feat_hbm, panel.at[own_rows, :], 0, at_row(peer * 2 + side), hop_sem.at[d])
    send(feat_hbm, panel.at[own_rows, :], 7, at_row(sibling))

    for copy in slot_loads:
        copy.wait()
    count = counts_ref[0, 0]
    group = 2 if col_tiles % 2 == 0 else 1
    groups = row_tiles * col_tiles // group

    def densify(tile_row, first_col, start, steps):
        gains = []
        for k in range(slots):
            live = jnp.logical_and(k < count, rows_ref[0, 0, k] == tile_row)
            col = cols_ref[0, 0, k]
            gains.append([
                jnp.where(jnp.logical_and(live, col == first_col + g), 1.0, 0.0).astype(F32)
                for g in range(group)
            ])

        def step(i, carry):
            at = pl.multiple_of(start + i * CHUNK, CHUNK)
            totals = [jnp.zeros((CHUNK, tile_len), F32) for _ in range(group)]
            for k in range(slots):
                block = tile_buf[k, pl.ds(at, CHUNK), :].astype(F32)
                totals = [total + block * gains[k][g] for g, total in enumerate(totals)]
            for g, total in enumerate(totals):
                rows = pl.ds(pl.multiple_of(tile_row * tile_len + at, CHUNK), CHUNK)
                lanes = pl.ds(pl.multiple_of((first_col + g) * tile_len, tile_len), tile_len)
                adj[rows, lanes] = total.astype(BF16)
            return carry

        lax.fori_loop(0, steps, step, 0)

    if groups == 1:
        for j in range(tile_parts):
            tile_loads[j].wait()
            densify(0, 0, j * part_rows, part_rows // CHUNK)
    else:
        for j in range(tile_parts):
            tile_loads[j].wait()

        def one_group(i, carry):
            per_row = col_tiles // group
            densify(i // per_row, lax.rem(i, per_row) * group, 0, tile_len // CHUNK)
            return carry

        lax.fori_loop(0, groups, one_group, 0)

    for copy in loads:
        copy.wait()
    for d in range(pairs - 1):
        source = lax.rem(pair + pairs - 1 - d, pairs) * 2 + side
        block = panel.at[pl.ds(pl.multiple_of(source * nodes, nodes), nodes), :]
        pltpu.make_async_copy(block, block, hop_sem.at[d]).wait()
        send(block, block, 7, at_row(sibling))
    wait_in(panel.at[pl.ds(0, pairs * nodes), :], 7)
    for c in range(n_col):
        part[c] = jnp.dot(
            adj[c * nodes:(c + 1) * nodes, :], panel[...], preferred_element_type=F32
        ).astype(BF16)
    for peer in col_peers:
        send(part.at[peer], part_in.at[my_col], 1, at_col(peer))
    part_in[my_col] = part[my_col]
    wait_in(part_in.at[pl.ds(0, n_col - 1)], 1)
    mixed = part_in[0].astype(F32)
    for c in range(1, n_col):
        mixed = mixed + part_in[c].astype(F32)
    mixed = mixed.astype(BF16)

    pre_act = jnp.dot(mixed, weight[...], preferred_element_type=F32) + bias[...]
    sig = jax.nn.sigmoid(pre_act)
    grad_pre = (cot[...].astype(F32) * (sig * (1.0 + pre_act * (1.0 - sig)))).astype(BF16)
    z_own = lax.dot_general(weight[...], grad_pre, (((1,), (1,)), ((), ())), preferred_element_type=F32)
    own_lanes = pl.ds(pl.multiple_of(my_col * nodes, nodes), nodes)
    z_buf[0:feat, own_lanes] = z_own.astype(BF16)
    gb_local = jnp.sum(grad_pre.astype(F32), axis=0, keepdims=True)
    halves = [gb_local[:, i * nodes:(i + 1) * nodes] for i in range(hidden // nodes)]
    n_half = len(halves)
    high = [half.astype(BF16).astype(F32) for half in halves]
    low = [half - top for half, top in zip(halves, high)]
    pad = jnp.zeros((EXTRA - 2 * n_half, nodes), F32)
    z_buf[feat:feat + EXTRA, own_lanes] = jnp.concatenate(high + low + [pad], axis=0).astype(BF16)
    for peer in col_peers:
        send(z_buf.at[:, own_lanes], z_buf.at[:, own_lanes], 2, at_col(peer))
    gw_local = lax.dot_general(mixed, grad_pre, (((0,), (0,)), ((), ())), preferred_element_type=F32)
    if fused_weight:
        share = feat // n_row
        gw_own[...] = gw_local.astype(BF16).reshape(n_row, share, hidden)
        for peer in row_peers:
            send(gw_own.at[peer], gw_in.at[my_row], 4, at_row(peer))
        gw_in[my_row] = gw_own[my_row]
    else:
        gw_st[...] = gw_local
    out_st[...] = (pre_act * sig).astype(BF16)

    wait_in(z_buf.at[:, pl.ds(0, (n_col - 1) * nodes)], 2)
    gb_block = z_buf[feat:feat + EXTRA, 0:nodes].astype(F32)
    for c in range(1, n_col):
        gb_block = gb_block + z_buf[feat:feat + EXTRA, c * nodes:(c + 1) * nodes].astype(F32)
    def split_rows(block):
        tops = [block[i:i + 1, :] + block[n_half + i:n_half + i + 1, :] for i in range(n_half)]
        rounded = [top.astype(BF16).astype(F32) for top in tops]
        rest = [top - near for top, near in zip(tops, rounded)]
        return jnp.concatenate(rounded + rest + [pad], axis=0).astype(BF16)

    for r in range(n_row):
        back[r % 2, r // 2, 0:feat, :] = jnp.dot(
            z_buf[0:feat, :], adj[:, r * nodes:(r + 1) * nodes], preferred_element_type=F32
        ).astype(BF16)
        back[r % 2, r // 2, feat:feat + EXTRA, :] = split_rows(gb_block)
    send(back.at[other], pair_in, 8, at_row(sibling))

    if fused_weight:
        wait_in(gw_in.at[pl.ds(0, n_row - 1)], 4)
        gw_sum = gw_in[0].astype(F32)
        for r in range(1, n_row):
            gw_sum = gw_sum + gw_in[r].astype(F32)
        gw_mid[my_col] = gw_sum.astype(BF16)
        for peer in col_peers:
            send(gw_mid.at[my_col], gw_mid.at[my_col], 5, at_col(peer))
    wait_in(pair_in, 8)
    back_out[:, 0:feat, :] = (
        back[side, :, 0:feat, :].astype(F32) + pair_in[:, 0:feat, :].astype(F32)
    ).astype(BF16)
    gb_pair = split_rows(gb_block + pair_in[0, feat:feat + EXTRA, :].astype(F32))
    for m in range(pairs):
        back_out[m, feat:feat + EXTRA, :] = gb_pair
    for peer in pair_peers:
        send(back_out.at[peer], back_in.at[pair], 3, at_row(peer * 2 + side))
    back_in[pair] = back_out[pair]
    if fused_weight:
        wait_in(gw_mid.at[pl.ds(0, n_col - 1)], 5)
        gw_sum = gw_mid[0].astype(F32)
        for c in range(1, n_col):
            gw_sum = gw_sum + gw_mid[c].astype(F32)
        gw_all[my_row] = gw_sum.astype(BF16)
        for peer in row_peers:
            send(gw_all.at[my_row], gw_all.at[my_row], 6, at_row(peer))

    wait_in(back_in.at[pl.ds(0, pairs - 1)], 3)
    total = back_in[0].astype(F32)
    for r in range(1, pairs):
        total = total + back_in[r].astype(F32)
    gf_st[...] = total[0:feat, :].T.astype(BF16)
    for i in range(n_half):
        gb_st[:, i * nodes:(i + 1) * nodes] = (
            total[feat + i:feat + i + 1, :] + total[feat + n_half + i:feat + n_half + i + 1, :]
        )
    if fused_weight:
        wait_in(gw_all.at[pl.ds(0, n_row - 1)], 6)
        gw_st[...] = gw_all[...].astype(F32).reshape(feat, hidden)

    wait_out(panel.at[pl.ds(0, (pairs - 1) * nodes), :], 0)
    wait_out(panel.at[pl.ds(0, pairs * nodes), :], 7)
    wait_out(part_in.at[pl.ds(0, n_col - 1)], 1)
    wait_out(z_buf.at[:, pl.ds(0, (n_col - 1) * nodes)], 2)
    wait_out(back_in.at[pl.ds(0, pairs - 1)], 3)
    wait_out(pair_in, 8)
    if fused_weight:
        wait_out(gw_in.at[pl.ds(0, n_row - 1)], 4)
        wait_out(gw_mid.at[pl.ds(0, n_col - 1)], 5)
        wait_out(gw_all.at[pl.ds(0, n_row - 1)], 6)


def shards(n_row, n_col, features, weight, bias, tiles, tile_rows, tile_cols, tile_counts, cotangent):
    nodes, feat = features.shape
    hidden = weight.shape[1]
    slots, tile_len = tiles.shape[2], tiles.shape[3]
    block_len, panel_len = nodes * n_col, nodes * n_row
    fused_weight = feat % (n_row * 16) == 0
    share = feat // n_row if fused_weight else 16
    hbm = pl.BlockSpec(memory_space=pltpu.HBM)
    vmem = pl.BlockSpec(memory_space=pltpu.VMEM)
    out, gf, gw, gb = pl.pallas_call(
        functools.partial(kernel, n_row, n_col, fused_weight),
        out_shape=(
            jax.ShapeDtypeStruct((nodes, hidden), BF16),
            jax.ShapeDtypeStruct((nodes, feat), BF16),
            jax.ShapeDtypeStruct((feat, hidden), F32),
            jax.ShapeDtypeStruct((1, hidden), F32),
        ),
        in_specs=[hbm] * 6 + [pl.BlockSpec(memory_space=pltpu.SMEM), hbm],
        out_specs=(vmem,) * 4,
        scratch_shapes=[
            pltpu.VMEM((slots, tile_len, tile_len), BF16),
            pltpu.VMEM((block_len, panel_len), BF16),
            pltpu.VMEM((panel_len, feat), BF16),
            pltpu.VMEM((feat, hidden), BF16),
            pltpu.VMEM((1, hidden), F32),
            pltpu.VMEM((nodes, hidden), BF16),
            pltpu.VMEM((n_col, nodes, feat), BF16),
            pltpu.VMEM((n_col, nodes, feat), BF16),
            pltpu.VMEM((feat + EXTRA, block_len), BF16),
            pltpu.VMEM((2, n_row // 2, feat + EXTRA, nodes), BF16),
            pltpu.VMEM((n_row // 2, feat + EXTRA, nodes), BF16),
            pltpu.VMEM((n_row // 2, feat + EXTRA, nodes), BF16),
            pltpu.VMEM((n_row // 2, feat + EXTRA, nodes), BF16),
            pltpu.VMEM((n_row, share, hidden), BF16),
            pltpu.VMEM((n_row, share, hidden), BF16),
            pltpu.VMEM((n_col, share, hidden), BF16),
            pltpu.VMEM((n_row, share, hidden), BF16),
            pltpu.SMEM(tile_rows.shape, jnp.int32),
            pltpu.SMEM(tile_cols.shape, jnp.int32),
            pltpu.SemaphoreType.DMA((4,)),
            pltpu.SemaphoreType.DMA((6,)),
            pltpu.SemaphoreType.DMA((9,)),
            pltpu.SemaphoreType.DMA((9,)),
            pltpu.SemaphoreType.DMA((n_row // 2,)),
        ],
        compiler_params=pltpu.CompilerParams(
            collective_id=0, has_side_effects=True, vmem_limit_bytes=48 * 1024 * 1024
        ),
    )(
        *[
            pltpu.with_memory_space_constraint(x, pltpu.HBM)
            for x in (features, weight, bias.reshape(1, hidden), tiles, tile_rows, tile_cols)
        ],
        tile_counts,
        pltpu.with_memory_space_constraint(cotangent, pltpu.HBM),
    )
    gb = gb.reshape(hidden)
    if not fused_weight:
        gw = lax.psum(gw, ("row", "col"))
    return out, gf, gw, gb


def solution(mesh):
    return jax.shard_map(
        functools.partial(shards, mesh.shape["row"], mesh.shape["col"]),
        mesh=mesh,
        in_specs=(
            P(("row", "col"), None),
            P(),
            P(),
            P("row", "col", None, None, None),
            P("row", "col", None),
            P("row", "col", None),
            P("row", "col"),
            P(("row", "col"), None),
        ),
        out_specs=(P(("row", "col"), None), P(("row", "col"), None), P(), P()),
        check_vma=False,
    )
```

```python
import functools

import jax
import jax.numpy as jnp
from jax import lax
from jax.experimental import pallas as pl
from jax.experimental.pallas import tpu as pltpu
from jax.sharding import PartitionSpec as P

F32, BF16 = jnp.float32, jnp.bfloat16
EXTRA = 16
CHUNK = 16


def kernel(
    n_row, n_col, fused_weight,
    feat_hbm, weight_hbm, bias_hbm, tiles_hbm, rows_hbm, cols_hbm, counts_ref, cot_hbm,
    out_st, gf_st, gw_st, gb_st,
    tile_buf, adj, panel, weight, bias, cot, part, part_in, z_buf, back, back_in,
    pair_in, back_out, gw_own, gw_in, gw_mid, gw_all,
    rows_ref, cols_ref, tile_sem, load_sem, send_sem, recv_sem, hop_sem,
):
    my_row, my_col = lax.axis_index("row"), lax.axis_index("col")
    nodes, feat = feat_hbm.shape
    hidden = weight.shape[1]
    slots, tile_len = tile_buf.shape[0], tile_buf.shape[1]
    row_tiles, col_tiles = adj.shape[0] // tile_len, adj.shape[1] // tile_len
    row_peers = [lax.rem(my_row + d, n_row) for d in range(1, n_row)]
    col_peers = [lax.rem(my_col + d, n_col) for d in range(1, n_col)]

    pairs = n_row // 2
    pair, side = my_row // 2, lax.rem(my_row, 2)
    other = 1 - side
    sibling = pair * 2 + other
    pair_peers = [lax.rem(pair + d, pairs) for d in range(1, pairs)]

    def at_row(peer):
        return (peer, my_col)

    def at_col(peer):
        return (my_row, peer)

    tile_parts = tile_sem.shape[0]
    part_rows = tile_len // tile_parts
    tile_loads = [
        pltpu.make_async_copy(
            tiles_hbm.at[0, 0, :, pl.ds(j * part_rows, part_rows), :],
            tile_buf.at[:, pl.ds(j * part_rows, part_rows), :],
            tile_sem.at[j],
        )
        for j in range(tile_parts)
    ]
    own_rows = pl.ds(pl.multiple_of(my_row * nodes, nodes), nodes)
    loads = [
        pltpu.make_async_copy(feat_hbm, panel.at[own_rows, :], load_sem.at[0]),
        pltpu.make_async_copy(weight_hbm, weight, load_sem.at[1]),
        pltpu.make_async_copy(bias_hbm, bias, load_sem.at[2]),
        pltpu.make_async_copy(cot_hbm, cot, load_sem.at[3]),
    ]
    slot_loads = [
        pltpu.make_async_copy(rows_hbm, rows_ref, load_sem.at[4]),
        pltpu.make_async_copy(cols_hbm, cols_ref, load_sem.at[5]),
    ]
    barrier = pltpu.get_barrier_semaphore()
    for peer in row_peers:
        pl.semaphore_signal(barrier, inc=1, device_id=at_row(peer), device_id_type=pl.DeviceIdType.MESH)
    for peer in col_peers:
        pl.semaphore_signal(barrier, inc=1, device_id=at_col(peer), device_id_type=pl.DeviceIdType.MESH)
    for copy in slot_loads + tile_loads + loads:
        copy.start()
    pl.semaphore_wait(barrier, n_row + n_col - 2)

    def send(src, dst, phase, target, landed=None):
        copy = pltpu.make_async_remote_copy(
            src_ref=src, dst_ref=dst, send_sem=send_sem.at[phase],
            recv_sem=recv_sem.at[phase] if landed is None else landed,
            device_id=target, device_id_type=pl.DeviceIdType.MESH,
        )
        copy.start()

    def wait_in(ref, phase):
        pltpu.make_async_copy(ref, ref, recv_sem.at[phase]).wait()

    def wait_out(ref, phase):
        pltpu.make_async_copy(ref, ref, send_sem.at[phase]).wait()

    for d, peer in enumerate(pair_peers):
        send(feat_hbm, panel.at[own_rows, :], 0, at_row(peer * 2 + side), hop_sem.at[d])
    send(feat_hbm, panel.at[own_rows, :], 7, at_row(sibling))

    for copy in slot_loads:
        copy.wait()
    count = counts_ref[0, 0]
    group = 2 if col_tiles % 2 == 0 else 1
    groups = row_tiles * col_tiles // group

    def densify(tile_row, first_col, start, steps):
        gains = []
        for k in range(slots):
            live = jnp.logical_and(k < count, rows_ref[0, 0, k] == tile_row)
            col = cols_ref[0, 0, k]
            gains.append([
                jnp.where(jnp.logical_and(live, col == first_col + g), 1.0, 0.0).astype(F32)
                for g in range(group)
            ])

        def step(i, carry):
            at = pl.multiple_of(start + i * CHUNK, CHUNK)
            totals = [jnp.zeros((CHUNK, tile_len), F32) for _ in range(group)]
            for k in range(slots):
                block = tile_buf[k, pl.ds(at, CHUNK), :].astype(F32)
                totals = [total + block * gains[k][g] for g, total in enumerate(totals)]
            for g, total in enumerate(totals):
                rows = pl.ds(pl.multiple_of(tile_row * tile_len + at, CHUNK), CHUNK)
                lanes = pl.ds(pl.multiple_of((first_col + g) * tile_len, tile_len), tile_len)
                adj[rows, lanes] = total.astype(BF16)
            return carry

        lax.fori_loop(0, steps, step, 0)

    if groups == 1:
        for j in range(tile_parts):
            tile_loads[j].wait()
            densify(0, 0, j * part_rows, part_rows // CHUNK)
    else:
        for j in range(tile_parts):
            tile_loads[j].wait()

        def one_group(i, carry):
            per_row = col_tiles // group
            densify(i // per_row, lax.rem(i, per_row) * group, 0, tile_len // CHUNK)
            return carry

        lax.fori_loop(0, groups, one_group, 0)

    for copy in loads:
        copy.wait()
    for d in range(pairs - 1):
        source = lax.rem(pair + pairs - 1 - d, pairs) * 2 + side
        block = panel.at[pl.ds(pl.multiple_of(source * nodes, nodes), nodes), :]
        pltpu.make_async_copy(block, block, hop_sem.at[d]).wait()
        send(block, block, 7, at_row(sibling))
    wait_in(panel.at[pl.ds(0, pairs * nodes), :], 7)
    for c in range(n_col):
        part[c] = jnp.dot(
            adj[c * nodes:(c + 1) * nodes, :], panel[...], preferred_element_type=F32
        ).astype(BF16)
    for peer in col_peers:
        send(part.at[peer], part_in.at[my_col], 1, at_col(peer))
    part_in[my_col] = part[my_col]
    wait_in(part_in.at[pl.ds(0, n_col - 1)], 1)
    mixed = part_in[0].astype(F32)
    for c in range(1, n_col):
        mixed = mixed + part_in[c].astype(F32)
    mixed = mixed.astype(BF16)

    pre_act = jnp.dot(mixed, weight[...], preferred_element_type=F32) + bias[...]
    sig = jax.nn.sigmoid(pre_act)
    grad_pre = (cot[...].astype(F32) * (sig * (1.0 + pre_act * (1.0 - sig)))).astype(BF16)
    z_own = lax.dot_general(weight[...], grad_pre, (((1,), (1,)), ((), ())), preferred_element_type=F32)
    own_lanes = pl.ds(pl.multiple_of(my_col * nodes, nodes), nodes)
    z_buf[0:feat, own_lanes] = z_own.astype(BF16)
    gb_local = jnp.sum(grad_pre.astype(F32), axis=0, keepdims=True)
    halves = [gb_local[:, i * nodes:(i + 1) * nodes] for i in range(hidden // nodes)]
    n_half = len(halves)
    high = [half.astype(BF16).astype(F32) for half in halves]
    low = [half - top for half, top in zip(halves, high)]
    pad = jnp.zeros((EXTRA - 2 * n_half, nodes), F32)
    z_buf[feat:feat + EXTRA, own_lanes] = jnp.concatenate(high + low + [pad], axis=0).astype(BF16)
    for peer in col_peers:
        send(z_buf.at[:, own_lanes], z_buf.at[:, own_lanes], 2, at_col(peer))
    gw_local = lax.dot_general(mixed, grad_pre, (((0,), (0,)), ((), ())), preferred_element_type=F32)
    if fused_weight:
        share = feat // n_row
        gw_own[...] = gw_local.astype(BF16).reshape(n_row, share, hidden)
        for peer in row_peers:
            send(gw_own.at[peer], gw_in.at[my_row], 4, at_row(peer))
        gw_in[my_row] = gw_own[my_row]
    else:
        gw_st[...] = gw_local
    out_st[...] = (pre_act * sig).astype(BF16)

    wait_in(z_buf.at[:, pl.ds(0, (n_col - 1) * nodes)], 2)
    gb_block = z_buf[feat:feat + EXTRA, 0:nodes].astype(F32)
    for c in range(1, n_col):
        gb_block = gb_block + z_buf[feat:feat + EXTRA, c * nodes:(c + 1) * nodes].astype(F32)
    def split_rows(block):
        tops = [block[i:i + 1, :] + block[n_half + i:n_half + i + 1, :] for i in range(n_half)]
        rounded = [top.astype(BF16).astype(F32) for top in tops]
        rest = [top - near for top, near in zip(tops, rounded)]
        return jnp.concatenate(rounded + rest + [pad], axis=0).astype(BF16)

    for r in range(n_row):
        back[r % 2, r // 2, 0:feat, :] = jnp.dot(
            z_buf[0:feat, :], adj[:, r * nodes:(r + 1) * nodes], preferred_element_type=F32
        ).astype(BF16)
        back[r % 2, r // 2, feat:feat + EXTRA, :] = split_rows(gb_block)
    send(back.at[other], pair_in, 8, at_row(sibling))

    if fused_weight:
        wait_in(gw_in.at[pl.ds(0, n_row - 1)], 4)
        gw_sum = gw_in[0].astype(F32)
        for r in range(1, n_row):
            gw_sum = gw_sum + gw_in[r].astype(F32)
        gw_mid[my_col] = gw_sum.astype(BF16)
        for peer in col_peers:
            send(gw_mid.at[my_col], gw_mid.at[my_col], 5, at_col(peer))
    wait_in(pair_in, 8)
    back_out[:, 0:feat, :] = (
        back[side, :, 0:feat, :].astype(F32) + pair_in[:, 0:feat, :].astype(F32)
    ).astype(BF16)
    gb_pair = split_rows(gb_block + pair_in[0, feat:feat + EXTRA, :].astype(F32))
    for m in range(pairs):
        back_out[m, feat:feat + EXTRA, :] = gb_pair
    for peer in pair_peers:
        send(back_out.at[peer], back_in.at[pair], 3, at_row(peer * 2 + side))
    back_in[pair] = back_out[pair]
    if fused_weight:
        wait_in(gw_mid.at[pl.ds(0, n_col - 1)], 5)
        gw_sum = gw_mid[0].astype(F32)
        for c in range(1, n_col):
            gw_sum = gw_sum + gw_mid[c].astype(F32)
        gw_all[my_row] = gw_sum.astype(BF16)
        for peer in row_peers:
            send(gw_all.at[my_row], gw_all.at[my_row], 6, at_row(peer))

    wait_in(back_in.at[pl.ds(0, pairs - 1)], 3)
    total = back_in[0].astype(F32)
    for r in range(1, pairs):
        total = total + back_in[r].astype(F32)
    gf_st[...] = total[0:feat, :].T.astype(BF16)
    for i in range(n_half):
        gb_st[:, i * nodes:(i + 1) * nodes] = (
            total[feat + i:feat + i + 1, :] + total[feat + n_half + i:feat + n_half + i + 1, :]
        )
    if fused_weight:
        wait_in(gw_all.at[pl.ds(0, n_row - 1)], 6)
        gw_st[...] = gw_all[...].astype(F32).reshape(feat, hidden)

    wait_out(panel.at[pl.ds(0, (pairs - 1) * nodes), :], 0)
    wait_out(panel.at[pl.ds(0, pairs * nodes), :], 7)
    wait_out(part_in.at[pl.ds(0, n_col - 1)], 1)
    wait_out(z_buf.at[:, pl.ds(0, (n_col - 1) * nodes)], 2)
    wait_out(back_in.at[pl.ds(0, pairs - 1)], 3)
    wait_out(pair_in, 8)
    if fused_weight:
        wait_out(gw_in.at[pl.ds(0, n_row - 1)], 4)
        wait_out(gw_mid.at[pl.ds(0, n_col - 1)], 5)
        wait_out(gw_all.at[pl.ds(0, n_row - 1)], 6)


def write_out(*refs):
    count = (len(refs) - 1) // 2
    sems = refs[-1]
    copies = [pltpu.make_async_copy(refs[i], refs[count + i], sems.at[i]) for i in range(count)]
    for copy in copies:
        copy.start()
    for copy in copies:
        copy.wait()


def shards(n_row, n_col, features, weight, bias, tiles, tile_rows, tile_cols, tile_counts, cotangent):
    nodes, feat = features.shape
    hidden = weight.shape[1]
    slots, tile_len = tiles.shape[2], tiles.shape[3]
    block_len, panel_len = nodes * n_col, nodes * n_row
    fused_weight = feat % (n_row * 16) == 0
    share = feat // n_row if fused_weight else 16
    hbm = pl.BlockSpec(memory_space=pltpu.HBM)
    vmem = pl.BlockSpec(memory_space=pltpu.VMEM)
    out, gf, gw, gb = pl.pallas_call(
        functools.partial(kernel, n_row, n_col, fused_weight),
        out_shape=(
            jax.ShapeDtypeStruct((nodes, hidden), BF16),
            jax.ShapeDtypeStruct((nodes, feat), BF16),
            jax.ShapeDtypeStruct((feat, hidden), F32),
            jax.ShapeDtypeStruct((1, hidden), F32),
        ),
        in_specs=[hbm] * 6 + [pl.BlockSpec(memory_space=pltpu.SMEM), hbm],
        out_specs=(vmem,) * 4,
        scratch_shapes=[
            pltpu.VMEM((slots, tile_len, tile_len), BF16),
            pltpu.VMEM((block_len, panel_len), BF16),
            pltpu.VMEM((panel_len, feat), BF16),
            pltpu.VMEM((feat, hidden), BF16),
            pltpu.VMEM((1, hidden), F32),
            pltpu.VMEM((nodes, hidden), BF16),
            pltpu.VMEM((n_col, nodes, feat), BF16),
            pltpu.VMEM((n_col, nodes, feat), BF16),
            pltpu.VMEM((feat + EXTRA, block_len), BF16),
            pltpu.VMEM((2, n_row // 2, feat + EXTRA, nodes), BF16),
            pltpu.VMEM((n_row // 2, feat + EXTRA, nodes), BF16),
            pltpu.VMEM((n_row // 2, feat + EXTRA, nodes), BF16),
            pltpu.VMEM((n_row // 2, feat + EXTRA, nodes), BF16),
            pltpu.VMEM((n_row, share, hidden), BF16),
            pltpu.VMEM((n_row, share, hidden), BF16),
            pltpu.VMEM((n_col, share, hidden), BF16),
            pltpu.VMEM((n_row, share, hidden), BF16),
            pltpu.SMEM(tile_rows.shape, jnp.int32),
            pltpu.SMEM(tile_cols.shape, jnp.int32),
            pltpu.SemaphoreType.DMA((4,)),
            pltpu.SemaphoreType.DMA((6,)),
            pltpu.SemaphoreType.DMA((9,)),
            pltpu.SemaphoreType.DMA((9,)),
            pltpu.SemaphoreType.DMA((n_row // 2,)),
        ],
        compiler_params=pltpu.CompilerParams(
            collective_id=0, has_side_effects=True, vmem_limit_bytes=48 * 1024 * 1024
        ),
    )(
        *[
            pltpu.with_memory_space_constraint(x, pltpu.HBM)
            for x in (features, weight, bias.reshape(1, hidden), tiles, tile_rows, tile_cols)
        ],
        tile_counts,
        pltpu.with_memory_space_constraint(cotangent, pltpu.HBM),
    )
    results = (out, gf, gw, gb)
    out, gf, gw, gb = pl.pallas_call(
        write_out,
        out_shape=tuple(jax.ShapeDtypeStruct(x.shape, x.dtype) for x in results),
        in_specs=[vmem] * 4,
        out_specs=(pl.BlockSpec(memory_space=pltpu.HBM),) * 4,
        scratch_shapes=[pltpu.SemaphoreType.DMA((4,))],
        compiler_params=pltpu.CompilerParams(vmem_limit_bytes=2 * 1024 * 1024),
    )(*results)
    gb = gb.reshape(hidden)
    if not fused_weight:
        gw = lax.psum(gw, ("row", "col"))
    return out, gf, gw, gb


def solution(mesh):
    return jax.shard_map(
        functools.partial(shards, mesh.shape["row"], mesh.shape["col"]),
        mesh=mesh,
        in_specs=(
            P(("row", "col"), None),
            P(),
            P(),
            P("row", "col", None, None, None),
            P("row", "col", None),
            P("row", "col", None),
            P("row", "col"),
            P(("row", "col"), None),
        ),
        out_specs=(P(("row", "col"), None), P(("row", "col"), None), P(), P()),
        check_vma=False,
    )
```
